32 devices in a mesh: dp: 4 (over z), block: 8 (over y, x, core).
Axes of the slice: x: 2, y: 2, z: 4, core: 2. Of those that a mesh axis runs over, the one named last changes fastest.
Arguments:
- tokens: bfloat16 [4096, 5120], P('dp', 'block'), may hold values from -6 to 6
- up_left: bfloat16 [128, 40, 160], P('block'), may hold values from -1 to 1
- up_right: bfloat16 [160, 128, 128], P('block'), may hold values from -0.5 to 0.5
- down_left: bfloat16 [160, 128, 128], P('block'), may hold values from -0.5 to 0.5
- down_right: bfloat16 [128, 160, 40], P('block'), may hold values from -0.5 to 0.5
- cotangent: bfloat16 [4096, 5120], P('dp', 'block'), may hold values from -6 to 6
Outputs:
- output: bfloat16 [4096, 5120], P('dp', 'block')
- grad_tokens: bfloat16 [4096, 5120], P('dp', 'block')
- grad_up_left: float32 [128, 40, 160], P('block')
- grad_up_right: float32 [160, 128, 128], P('block')
- grad_down_left: float32 [160, 128, 128], P('block')
- grad_down_right: float32 [128, 160, 40], P('block')
The draws below stay inside these ranges and needn't reach their ends.
All inputs are finite; a program needn't handle non-finite values.
Results may differ from the reference program's by a relative error of at most 0.007.
Values may be sent and summed in bfloat16 or wider, within the bound.
A program may use at most 192 MiB of HBM per device.

```python
import jax
import jax.numpy as jnp
from jax import lax

D = 5120
FF = 20480
BS = 128
MB = 160
AW = 40
TOKENS = 4096
N_DP = 4


def shard_levels(own_key, extent, shards, smallest, largest):
    loudness, own = 1.0, jax.random.fold_in(own_key, 6)
    for position, shards_of in shards:
        steps = jnp.exp(jax.random.uniform(jax.random.fold_in(own, position), (shards_of,), jnp.float32, smallest / len(shards), largest / len(shards)))
        loudness = loudness * jnp.repeat(steps, extent[position] // shards_of).reshape([-1 if axis == position else 1 for axis in range(len(extent))])
    return loudness


def centred(rng, extent, spread, limit, split=(), kind=jnp.bfloat16):
    array = jax.random.normal(rng, extent, jnp.float32) * spread
    if len(split) > 0:
        array = shard_levels(rng, extent, split, -0.22, 0.18) * array
    return jnp.clip(array, min=-limit, max=limit).astype(kind)


def setup_inputs(seed: int = 0) -> dict:
    keys = jax.random.split(jax.random.key(seed), 7)
    tokens = centred(keys[0], (TOKENS, D), 1.0, 6.0, ((0, 4), (1, 8)))
    up_left = centred(keys[1], (BS, AW, MB), AW ** -0.5, 1.0, ((0, 8),))
    up_right = centred(keys[2], (MB, BS, BS), BS ** -0.5, 0.5, ((0, 8),))
    down_left = centred(keys[3], (MB, BS, BS), BS ** -0.5, 0.5, ((0, 8),))
    down_right = centred(keys[4], (BS, MB, AW), MB ** -0.5, 0.5, ((0, 8),))
    cotangent = centred(keys[5], (TOKENS, D), 1.0, 6.0, ((0, 4), (1, 8)))
    return dict(tokens=tokens, up_left=up_left, up_right=up_right, down_left=down_left, down_right=down_right, cotangent=cotangent)


root_half = 0.7071067811865476
gauss_norm = 0.3989422804014327


def gelu_exact(value):
    return 0.5 * value * (1.0 + lax.erf(value * root_half))


def gelu_slope(value):
    return 0.5 * (1.0 + lax.erf(value * root_half)) + value * jnp.exp(-0.5 * value * value) * gauss_norm


def reference(tokens, up_left, up_right, down_left, down_right, cotangent):
    rows = TOKENS // N_DP
    width_in = D // BS
    inputs = tokens.reshape(N_DP, rows, BS, width_in)
    grads_in = cotangent.reshape(N_DP, rows, BS, width_in)
    w_first = up_left.astype(jnp.float32)
    w_second = up_right.astype(jnp.float32)
    w_third = down_left.astype(jnp.float32)
    w_fourth = down_right.astype(jnp.float32)

    def group_step(carry, pair):
        acc_ul, acc_ur, acc_dl, acc_dr = carry
        xin, cot = pair
        xin_f = xin.astype(jnp.float32)
        cot_f = cot.astype(jnp.float32)
        first = jnp.einsum("tia,iaj->tji", xin_f, w_first).astype(jnp.bfloat16)
        pre_act = jnp.einsum("tji,jim->tjm", first.astype(jnp.float32), w_second)
        hidden = gelu_exact(pre_act).astype(jnp.bfloat16)
        second = jnp.einsum("tjk,jkl->tlj", hidden.astype(jnp.float32), w_third).astype(jnp.bfloat16)
        output = jnp.einsum("tlj,ljo->tlo", second.astype(jnp.float32), w_fourth).astype(jnp.bfloat16)
        grad_dr = jnp.einsum("tlj,tlo->ljo", second.astype(jnp.float32), cot_f)
        grad_second = jnp.einsum("tlo,ljo->tlj", cot_f, w_fourth).astype(jnp.bfloat16)
        grad_second_f = grad_second.astype(jnp.float32)
        grad_dl = jnp.einsum("tjk,tlj->jkl", hidden.astype(jnp.float32), grad_second_f)
        grad_hidden = jnp.einsum("tlj,jkl->tjk", grad_second_f, w_third)
        grad_pre = (grad_hidden * gelu_slope(pre_act)).astype(jnp.bfloat16)
        grad_pre_f = grad_pre.astype(jnp.float32)
        grad_ur = jnp.einsum("tji,tjm->jim", first.astype(jnp.float32), grad_pre_f)
        grad_first = jnp.einsum("tjm,jim->tji", grad_pre_f, w_second).astype(jnp.bfloat16)
        grad_first_f = grad_first.astype(jnp.float32)
        grad_ul = jnp.einsum("tia,tji->iaj", xin_f, grad_first_f)
        grad_x = jnp.einsum("tji,iaj->tia", grad_first_f, w_first).astype(jnp.bfloat16)
        carry = (acc_ul + grad_ul, acc_ur + grad_ur, acc_dl + grad_dl, acc_dr + grad_dr)
        return carry, (output, grad_x)

    init = (jnp.zeros((BS, width_in, FF // BS), jnp.float32),
            jnp.zeros((FF // BS, BS, BS), jnp.float32),
            jnp.zeros((FF // BS, BS, BS), jnp.float32),
            jnp.zeros((BS, FF // BS, width_in), jnp.float32))
    sums, stacked = lax.scan(group_step, init, (inputs, grads_in))
    output = stacked[0].reshape(TOKENS, D)
    grad_tokens = stacked[1].reshape(TOKENS, D)
    return output, grad_tokens, sums[0], sums[1], sums[2], sums[3]
```

```python
import jax
import jax.numpy as jnp
from jax import lax
from jax.sharding import PartitionSpec as P

root_half = 0.7071067811865476
gauss_norm = 0.3989422804014327
F32, BF16 = jnp.float32, jnp.bfloat16


def gelu_exact(value):
    return 0.5 * value * (1.0 + lax.erf(value * root_half))


def gelu_slope(value):
    return (
        0.5 * (1.0 + lax.erf(value * root_half))
        + value * jnp.exp(-0.5 * value * value) * gauss_norm
    )


def mul(spec, a, b):
    return jnp.einsum(spec, a, b, preferred_element_type=F32)


def swap(piece, n, bit):
    return lax.ppermute(piece, "block", [(d, d ^ bit) for d in range(n)])


def orders(n):
    bits = [1 << p for p in range(1, n.bit_length() - 1)]
    return bits, bits[::-1]


def gather(halves, n):
    have = [{0: half} for half in halves]
    for step in range(len(orders(n)[0])):
        for h, order in enumerate(orders(n)):
            for k in sorted(have[h]):
                have[h][k ^ order[step]] = swap(have[h][k], n, order[step])
    for h in range(2):
        for k in list(have[h]):
            have[h][k ^ 1] = swap(have[h][k], n, 1)
    return have


def scatter(parts, n):
    def fold(pieces, bit):
        return {
            k: (pieces[k].astype(F32) + swap(pieces[k ^ bit], n, bit).astype(F32)).astype(BF16)
            for k in sorted(pieces)
            if not k & bit
        }

    now = [fold(pieces, 1) for pieces in parts]
    for step in range(len(orders(n)[0])):
        now = [fold(now[h], order[step]) for h, order in enumerate(orders(n))]
    return jnp.concatenate([now[0][0], now[1][0]], axis=0)


def make_on_device(n):
    def on_device(tokens, up_left, up_right, down_left, down_right, cotangent):
        me = lax.axis_index("block")
        rows = tokens.shape[0]
        bi, aw, mb = up_left.shape
        own, bs, half = mb // n, up_right.shape[1], bi // 2
        xt = tokens.T.reshape(bi, aw, rows)
        ct = cotangent.T.reshape(bi, aw, rows)

        outer = jnp.stack([jnp.transpose(up_left, (0, 2, 1)), down_right])
        outer = jnp.transpose(outer.reshape(2 * bi, n, own * aw), (1, 0, 2))
        outer = lax.all_to_all(outer, "block", split_axis=0, concat_axis=0, tiled=True)
        outer = [
            lax.dynamic_index_in_dim(outer, me ^ k, 0, keepdims=False).reshape(2, bi, own, aw)
            for k in range(n)
        ]
        index = jnp.arange(bs)
        target = ((index // bi) ^ me) * bi + index % bi
        perm = (index[:, None] == target[None, :]).astype(BF16)
        ur = mul("jim,ip->jpm", up_right, perm).astype(BF16)
        dl = mul("jkl,lp->jkp", down_left, perm).astype(BF16)

        x = gather((xt[:half], xt[half:]), n)
        ct, *_ = lax.optimization_barrier(
            (ct, x[0][orders(n)[0][0]], x[1][orders(n)[1][0]])
        )
        c = gather((ct[:half], ct[half:]), n)

        def outer_of(which, h, k):
            return outer[k][which, h * half : (h + 1) * half]

        def cut(array, h, k):
            return array[k * bi + h * half : k * bi + (h + 1) * half]

        def every(make):
            return jnp.concatenate([make(h, k) for k in range(n) for h in range(2)], axis=0)

        first = every(lambda h, k: mul("iat,ija->ijt", x[h][k], outer_of(0, h, k)).astype(BF16))
        pre_act = mul("ijt,jim->jmt", first, ur)
        hidden = gelu_exact(pre_act).astype(BF16)
        second = mul("jkt,jkl->ljt", hidden, dl).astype(BF16)
        out = [
            {
                k: mul("ljt,ljo->lot", cut(second, h, k), outer_of(1, h, k)).astype(BF16)
                for k in range(n)
            }
            for h in range(2)
        ]
        output = scatter(out, n).reshape(bi * aw, rows).T

        grad_second = every(
            lambda h, k: mul("lot,ljo->ljt", c[h][k], outer_of(1, h, k)).astype(BF16)
        )
        grad_hidden = mul("ljt,jkl->jkt", grad_second, dl)
        grad_pre = (grad_hidden * gelu_slope(pre_act)).astype(BF16)
        grad_first = mul("jmt,jim->ijt", grad_pre, ur).astype(BF16)
        gx = [
            {
                k: mul("ijt,ija->iat", cut(grad_first, h, k), outer_of(0, h, k)).astype(BF16)
                for k in range(n)
            }
            for h in range(2)
        ]
        grad_x = scatter(gx, n).reshape(bi * aw, rows).T

        grad_dl = mul("jkt,ljt->jkl", hidden, grad_second).astype(BF16)
        grad_ur = mul("ijt,jmt->jim", first, grad_pre).astype(BF16)
        grad_dl = mul("jkp,lp->jkl", grad_dl, perm).astype(BF16)
        grad_ur = mul("jpm,ip->jim", grad_ur, perm).astype(BF16)
        grad_dl, grad_ur = lax.psum((grad_dl, grad_ur), "dp")
        grad_dr = every(lambda h, k: mul("ljt,lot->ljo", cut(second, h, k), c[h][k]).astype(BF16))
        grad_ul = every(
            lambda h, k: mul("ijt,iat->ija", cut(grad_first, h, k), x[h][k]).astype(BF16)
        )
        both = jnp.concatenate(
            [grad_ul.reshape(n, bi, own * aw), grad_dr.reshape(n, bi, own * aw)], axis=1
        )
        both = jnp.concatenate(
            [lax.dynamic_index_in_dim(both, me ^ k, 0, keepdims=True) for k in range(n)], axis=0
        )
        both = lax.all_to_all(both, "block", split_axis=0, concat_axis=0, tiled=True)
        both = lax.psum(both, "dp").astype(F32).reshape(n, 2, bi, own, aw)
        grad_ul = jnp.transpose(both[:, 0], (1, 3, 0, 2)).reshape(bi, aw, mb)
        grad_dr = jnp.transpose(both[:, 1], (1, 0, 2, 3)).reshape(bi, mb, aw)
        return (output, grad_x, grad_ul, grad_ur.astype(F32), grad_dl.astype(F32), grad_dr)

    return on_device


def solution(mesh):
    return jax.shard_map(
        make_on_device(mesh.shape["block"]),
        mesh=mesh,
        in_specs=(
            P("dp", "block"),
            P("block", None, None),
            P("block", None, None),
            P("block", None, None),
            P("block", None, None),
            P("dp", "block"),
        ),
        out_specs=(
            P("dp", "block"),
            P("dp", "block"),
            P("block", None, None),
            P("block", None, None),
            P("block", None, None),
            P("block", None, None),
        ),
        check_vma=False,
    )
```

```python
import functools

import jax
import jax.numpy as jnp
from jax import lax
from jax.experimental import pallas as pl
from jax.experimental.pallas import tpu as pltpu
from jax.sharding import PartitionSpec as P

root_half = 0.7071067811865476
gauss_norm = 0.3989422804014327
F32, BF16 = jnp.float32, jnp.bfloat16
TILE = 256
WHOLE = pl.BlockSpec(memory_space=pltpu.VMEM)
PARAMS = pltpu.CompilerParams(vmem_limit_bytes=56 * 1024 * 1024)


def mul(spec, a, b):
    return jnp.einsum(spec, a, b, preferred_element_type=F32)


def dot(a, b):
    return jnp.dot(a, b, preferred_element_type=F32)


def dot_rows(a, b):
    return lax.dot_general(a, b, (((1,), (1,)), ((), ())), preferred_element_type=F32)


def swap(piece, n, bit):
    return lax.ppermute(piece, "block", [(d, d ^ bit) for d in range(n)])


def orders(n):
    bits = [1 << p for p in range(1, n.bit_length() - 1)]
    return bits, bits[::-1]


def sequence(n, h):
    seq = [0]
    for bit in orders(n)[h][::-1]:
        seq = seq + [k ^ bit for k in seq]
    return seq


def gather(halves, n):
    have = [{0: half} for half in halves]
    for step in range(len(orders(n)[0])):
        for h, order in enumerate(orders(n)):
            for k in sorted(have[h]):
                have[h][k ^ order[step]] = swap(have[h][k], n, order[step])
    for h in range(2):
        for k in list(have[h]):
            have[h][k ^ 1] = swap(have[h][k], n, 1)
    return have


def fold(kept, sent, n, bit):
    return (kept.astype(F32) + swap(sent, n, bit).astype(F32)).astype(BF16)


def scatter(even, odd, n, h):
    now = fold(even, odd, n, 1)
    for bit in orders(n)[h]:
        middle = now.shape[0] // 2
        now = fold(now[:middle], now[middle:], n, bit)
    return now[0]


def sum_groups(rows, m):
    me = lax.axis_index("dp")
    parts = rows.reshape(m, -1, rows.shape[1])

    def pick(s):
        return lax.dynamic_index_in_dim(parts, lax.rem(me + s, m), 0, keepdims=False)

    def shift(value, s):
        return lax.ppermute(value, "dp", [(d, (d + s) % m) for d in range(m)])

    total = pick(0).astype(F32)
    for got in [shift(pick(s), s) for s in range(1, m)]:
        total = total + got.astype(F32)
    total = total.astype(BF16)
    result = parts
    for s, got in enumerate([total] + [shift(total, s) for s in range(1, m)]):
        result = lax.dynamic_update_index_in_dim(result, got, lax.rem(me + m - s, m), 0)
    return result.reshape(rows.shape)


def forward_kernel(n, bi, own, seq, *refs):
    x = refs[:n]
    wf, wd, urt, dlt, first, slope, hidden, outer, even, odd, sa, sb = refs[n:]
    width = first.shape[2]
    for k in range(n):
        sa[:, k * bi : (k + 1) * bi, :] = dot(wf[k], x[k][...]).reshape(own, bi, width)

    def step(j, carry):
        entry = sa[j].astype(BF16)
        first[j] = entry
        pre = dot(urt[j], entry)
        cdf = 0.5 * (1.0 + lax.erf(pre * root_half))
        slope[j] = cdf + pre * jnp.exp(-0.5 * pre * pre) * gauss_norm
        act = (pre * cdf).astype(BF16)
        hidden[j] = act
        sb[j] = dot(dlt[j], act)
        return carry

    lax.fori_loop(0, own, step, 0, unroll=2)
    for k in range(n):
        piece = sb[:, k * bi : (k + 1) * bi, :].reshape(own * bi, width).astype(BF16)
        outer[k] = piece
        (odd if k & 1 else even)[seq.index(k & ~1)] = dot(wd[k], piece).astype(BF16)


def backward_kernel(n, bi, own, seq, *refs):
    c = refs[:n]
    wf, wd, ur, dl, first, slope, hidden, gdl, gur, outer, even, odd, sa, sb = refs[n:]
    width = first.shape[2]

    @pl.when(pl.program_id(0) == 0)
    def _():
        gdl[...] = jnp.zeros_like(gdl)
        gur[...] = jnp.zeros_like(gur)

    for k in range(n):
        sa[:, k * bi : (k + 1) * bi, :] = dot(wf[k], c[k][...]).reshape(own, bi, width)

    def step(j, carry):
        entry = sa[j].astype(BF16)
        gdl[j] += dot_rows(hidden[j], entry)
        grad_pre = (dot(dl[j], entry) * slope[j]).astype(BF16)
        gur[j] += dot_rows(first[j], grad_pre)
        sb[j] = dot(ur[j], grad_pre)
        return carry

    lax.fori_loop(0, own, step, 0, unroll=2)
    for k in range(n):
        piece = sb[:, k * bi : (k + 1) * bi, :].reshape(own * bi, width).astype(BF16)
        outer[k] = piece
        (odd if k & 1 else even)[seq.index(k & ~1)] = dot(wd[k], piece).astype(BF16)


def outer_kernel(n, per_half, *refs):
    x, c = (refs[:n], refs[n : 2 * n]), (refs[2 * n : 3 * n], refs[3 * n : 4 * n])
    gf, second = refs[4 * n : 4 * n + 2], refs[4 * n + 2 : 4 * n + 4]
    mask, select, out, acc_x, acc_c = refs[4 * n + 4 :]
    tile = pl.program_id(0)

    @pl.when(tile == 0)
    def _():
        acc_x[...] = jnp.zeros_like(acc_x)
        acc_c[...] = jnp.zeros_like(acc_c)

    for h in range(2):

        @pl.when(tile // per_half == h)
        def _():
            for k in range(n):
                acc_x[k] += dot_rows(gf[h][k], x[h][k][...])
                acc_c[k] += dot_rows(second[h][k], c[h][k][...])

    @pl.when(tile == 2 * per_half - 1)
    def _():
        for k in range(n):
            kept = mask[...]
            out[k] = (
                dot((acc_x[k] * kept).astype(BF16), select[0])
                + dot((acc_c[k] * kept).astype(BF16), select[1])
            ).astype(BF16)


def make_on_device(n, m):
    def on_device(tokens, up_left, up_right, down_left, down_right, cotangent):
        me = lax.axis_index("block")
        rows = tokens.shape[0]
        bi, aw, mb = up_left.shape
        own, bs = mb // n, up_right.shape[1]
        piece, ends, span = own * bi, bi * aw, rows // 2
        tiles = span // TILE

        outer = jnp.concatenate(
            [jnp.transpose(up_left, (2, 0, 1)), jnp.transpose(down_right, (1, 0, 2))], axis=2
        ).reshape(n, piece, 2 * aw)
        outer = lax.all_to_all(outer, "block", split_axis=0, concat_axis=0, tiled=True)
        outer = jnp.concatenate(
            [lax.dynamic_index_in_dim(outer, me ^ k, 0) for k in range(n)], axis=0
        )
        lane, row = jnp.arange(ends), jnp.arange(piece)
        mask = row[:, None] % bi == lane[None, :] // aw
        spread = lane[None, :] % aw == jnp.arange(2 * aw)[:, None] - jnp.array([[[0]], [[aw]]])
        spread = spread.astype(BF16)
        wide = mul("krb,zbc->zkrc", outer, spread).astype(BF16) * mask.astype(BF16)
        tall = jnp.transpose(wide, (0, 1, 3, 2))
        select = jnp.transpose(spread, (0, 2, 1))
        index = jnp.arange(bs)
        target = ((index // bi) ^ me) * bi + index % bi
        perm = (index[:, None] == target[None, :]).astype(BF16)
        ur = mul("jim,ip->jpm", up_right, perm).astype(BF16)
        dl = mul("jkl,lp->jkp", down_left, perm).astype(BF16)
        urt, dlt = jnp.transpose(ur, (0, 2, 1)), jnp.transpose(dl, (0, 2, 1))

        xt, ct = tokens.T, cotangent.T
        x = gather((xt[:, :span], xt[:, span:]), n)
        ct, *_ = lax.optimization_barrier(
            (ct, x[0][orders(n)[0][0]], x[1][orders(n)[1][0]])
        )
        c = gather((ct[:, :span], ct[:, span:]), n)

        ends_in = pl.BlockSpec((ends, TILE), lambda t: (0, t))
        middle = pl.BlockSpec((own, bs, TILE), lambda t: (0, 0, t))
        outside = pl.BlockSpec((n, piece, TILE), lambda t: (0, 0, t))
        parts = pl.BlockSpec((n // 2, ends, TILE), lambda t: (0, 0, t))
        square = pl.BlockSpec((own, bs, bs), lambda t: (0, 0, 0))
        middle_of = lambda kind: jax.ShapeDtypeStruct((own, bs, span), kind)
        outside_of = jax.ShapeDtypeStruct((n, piece, span), BF16)
        parts_of = jax.ShapeDtypeStruct((n // 2, ends, span), BF16)
        square_of = jax.ShapeDtypeStruct((own, bs, bs), F32)
        scratch = [pltpu.VMEM((own, bs, TILE), F32)] * 2
        flops = 2 * n * 2 * piece * ends * span + 4 * own * bs * bs * span
        cost = pl.CostEstimate(flops=flops, bytes_accessed=30_000_000, transcendentals=0)

        first, slope, hidden, second, output = [], [], [], [], []
        for h in range(2):
            a, b, e, s, even, odd = pl.pallas_call(
                functools.partial(forward_kernel, n, bi, own, sequence(n, h)),
                grid=(tiles,),
                in_specs=[ends_in] * n + [WHOLE] * 4,
                out_specs=[middle, middle, middle, outside, parts, parts],
                out_shape=[
                    middle_of(BF16), middle_of(F32), middle_of(BF16), outside_of, parts_of, parts_of
                ],
                scratch_shapes=scratch,
                compiler_params=PARAMS,
                cost_estimate=cost,
                name="forward_chain",
            )(*[x[h][k] for k in range(n)], wide[0], tall[1], urt, dlt)
            first.append(a)
            slope.append(b)
            hidden.append(e)
            second.append(s)
            output.append(scatter(even, odd, n, h))

        grad_dl, grad_ur, grad_first, grad_x = [], [], [], []
        for h in range(2):
            a, b, s, even, odd = pl.pallas_call(
                functools.partial(backward_kernel, n, bi, own, sequence(n, h)),
                grid=(tiles,),
                in_specs=[ends_in] * n + [WHOLE] * 4 + [middle] * 3,
                out_specs=[square, square, outside, parts, parts],
                out_shape=[square_of, square_of, outside_of, parts_of, parts_of],
                scratch_shapes=scratch,
                compiler_params=PARAMS,
                cost_estimate=cost,
                name="backward_chain",
            )(*[c[h][k] for k in range(n)], wide[1], tall[0], ur, dl, first[h], slope[h], hidden[h])
            grad_dl.append(a)
            grad_ur.append(b)
            grad_first.append(s)
            grad_x.append(scatter(even, odd, n, h))

        grad_dl = mul("jkp,lp->jkl", (grad_dl[0] + grad_dl[1]).astype(BF16), perm).astype(BF16)
        grad_ur = mul("jpm,ip->jim", (grad_ur[0] + grad_ur[1]).astype(BF16), perm).astype(BF16)
        square_sum = sum_groups(
            jnp.concatenate([grad_dl.reshape(-1, bs), grad_ur.reshape(-1, bs)], axis=0), m
        ).astype(F32).reshape(2, own, bs, bs)

        ends_at = [
            pl.BlockSpec((ends, TILE), lambda t: (0, jnp.minimum(t, tiles - 1))),
            pl.BlockSpec((ends, TILE), lambda t: (0, jnp.maximum(t - tiles, 0))),
        ]
        outside_at = [
            pl.BlockSpec((n, piece, TILE), lambda t: (0, 0, jnp.minimum(t, tiles - 1))),
            pl.BlockSpec((n, piece, TILE), lambda t: (0, 0, jnp.maximum(t - tiles, 0))),
        ]
        both = pl.pallas_call(
            functools.partial(outer_kernel, n, tiles),
            grid=(2 * tiles,),
            in_specs=([ends_at[0]] * n + [ends_at[1]] * n) * 2 + outside_at * 2 + [WHOLE] * 2,
            out_specs=pl.BlockSpec((n, piece, 2 * aw), lambda t: (0, 0, 0)),
            out_shape=jax.ShapeDtypeStruct((n, piece, 2 * aw), BF16),
            scratch_shapes=[pltpu.VMEM((n, piece, ends), F32)] * 2,
            compiler_params=PARAMS,
            cost_estimate=cost,
            name="outer_gradients",
        )(
            *[x[h][k] for h in range(2) for k in range(n)],
            *[c[h][k] for h in range(2) for k in range(n)],
            *grad_first, *second, mask.astype(F32), select,
        )
        both = jnp.concatenate(
            [lax.dynamic_index_in_dim(both, me ^ k, 0) for k in range(n)], axis=0
        )
        both = lax.all_to_all(both, "block", split_axis=0, concat_axis=0, tiled=True)
        both = sum_groups(both.reshape(n * piece, 2 * aw), m).reshape(mb, bi, 2 * aw).astype(F32)
        return (
            jnp.concatenate(output, axis=1).T,
            jnp.concatenate(grad_x, axis=1).T,
            jnp.transpose(both[:, :, :aw], (1, 2, 0)),
            square_sum[1],
            square_sum[0],
            jnp.transpose(both[:, :, aw:], (1, 0, 2)),
        )

    return on_device


def solution(mesh):
    return jax.shard_map(
        make_on_device(mesh.shape["block"], mesh.shape["dp"]),
        mesh=mesh,
        in_specs=(
            P("dp", "block"),
            P("block", None, None),
            P("block", None, None),
            P("block", None, None),
            P("block", None, None),
            P("dp", "block"),
        ),
        out_specs=(
            P("dp", "block"),
            P("dp", "block"),
            P("block", None, None),
            P("block", None, None),
            P("block", None, None),
            P("block", None, None),
        ),
        check_vma=False,
    )
```

```python
import functools

import jax
import jax.numpy as jnp
from jax import lax
from jax.experimental import pallas as pl
from jax.experimental.pallas import tpu as pltpu
from jax.sharding import PartitionSpec as P

root_half = 0.7071067811865476
gauss_norm = 0.3989422804014327
F32, BF16 = jnp.float32, jnp.bfloat16
TILE = 256
WHOLE = pl.BlockSpec(memory_space=pltpu.VMEM)
PARAMS = pltpu.CompilerParams(vmem_limit_bytes=56 * 1024 * 1024)


def mul(spec, a, b):
    return jnp.einsum(spec, a, b, preferred_element_type=F32)


def dot(a, b):
    return jnp.dot(a, b, preferred_element_type=F32)


def dot_rows(a, b):
    return lax.dot_general(a, b, (((1,), (1,)), ((), ())), preferred_element_type=F32)


def swap(piece, n, bit):
    return lax.ppermute(piece, "block", [(d, d ^ bit) for d in range(n)])


def orders(n):
    bits = [1 << p for p in range(1, n.bit_length() - 1)]
    return bits, bits[::-1]


def sequence(n, h):
    seq = [0]
    for bit in orders(n)[h][::-1]:
        seq = seq + [k ^ bit for k in seq]
    return seq


def gather(halves, n):
    have = [{0: half} for half in halves]
    for step in range(len(orders(n)[0])):
        for h, order in enumerate(orders(n)):
            for k in sorted(have[h]):
                have[h][k ^ order[step]] = swap(have[h][k], n, order[step])
    for h in range(2):
        for k in list(have[h]):
            have[h][k ^ 1] = swap(have[h][k], n, 1)
    return have


def fold(kept, sent, n, bit):
    return (kept.astype(F32) + swap(sent, n, bit).astype(F32)).astype(BF16)


def scatter_step(now, n, bit):
    middle = now.shape[0] // 2
    return fold(now[:middle], now[middle:], n, bit)


def sum_groups(rows, m):
    me = lax.axis_index("dp")
    bits = [1 << p for p in range(m.bit_length() - 1)]

    def trade(value, bit):
        return lax.ppermute(value, "dp", [(d, d ^ bit) for d in range(m)])

    def halve(value, bit):
        side = lax.rem(me // bit, 2)
        size = value.shape[0] // 2
        kept = lax.dynamic_slice_in_dim(value, side * size, size, 0)
        sent = lax.dynamic_slice_in_dim(value, (1 - side) * size, size, 0)
        return (kept.astype(F32) + trade(sent, bit).astype(F32)).astype(BF16)

    def finish(value):
        for bit in bits[1:]:
            value = halve(value, bit)
        for bit in bits[::-1]:
            got, low = trade(value, bit), lax.rem(me // bit, 2) == 0
            value = jnp.concatenate([jnp.where(low, value, got), jnp.where(low, got, value)])
        return value

    return halve(rows, bits[0]), finish


def build(n, which_in, which_out, outer, spread, tall_spread, mask, tall_mask, wf, wd):
    me = lax.axis_index("block")
    for k in range(n):
        block = outer[me ^ k]
        wf[k] = dot(block, spread[which_in]).astype(BF16) * mask[...]
        wd[k] = dot_rows(tall_spread[which_out], block).astype(BF16) * tall_mask[...]


def forward_kernel(n, bi, own, seq, *refs):
    x = refs[:n]
    outer_in, spread, tall_spread, mask, tall_mask, urt, dlt = refs[n : n + 7]
    first, slope, hidden, outer, even, odd, sa, sb, wf, wd = refs[-10:]
    width = first.shape[2]

    @pl.when(pl.program_id(0) == 0)
    def _():
        build(n, 0, 1, outer_in, spread, tall_spread, mask, tall_mask, wf, wd)

    for k in range(n):
        sa[:, k * bi : (k + 1) * bi, :] = dot(wf[k], x[k][...]).reshape(own, bi, width)

    def step(j, carry):
        entry = sa[j].astype(BF16)
        first[j] = entry
        pre = dot(urt[j], entry)
        cdf = 0.5 * (1.0 + lax.erf(pre * root_half))
        slope[j] = cdf + pre * jnp.exp(-0.5 * pre * pre) * gauss_norm
        act = (pre * cdf).astype(BF16)
        hidden[j] = act
        sb[j] = dot(dlt[j], act)
        return carry

    lax.fori_loop(0, own, step, 0, unroll=2)
    for k in range(n):
        piece = sb[:, k * bi : (k + 1) * bi, :].reshape(own * bi, width).astype(BF16)
        outer[k] = piece
        (odd if k & 1 else even)[seq.index(k & ~1)] = dot(wd[k], piece).astype(BF16)


def backward_kernel(n, bi, own, seq, *refs):
    c = refs[:n]
    outer_in, spread, tall_spread, mask, tall_mask, ur, dl, first, slope, hidden = refs[n : n + 10]
    gdl, gur, outer, even, odd, sa, sb, wf, wd = refs[-9:]
    width = first.shape[2]

    @pl.when(pl.program_id(0) == 0)
    def _():
        gdl[...] = jnp.zeros_like(gdl)
        gur[...] = jnp.zeros_like(gur)
        build(n, 1, 0, outer_in, spread, tall_spread, mask, tall_mask, wf, wd)

    for k in range(n):
        sa[:, k * bi : (k + 1) * bi, :] = dot(wf[k], c[k][...]).reshape(own, bi, width)

    def step(j, carry):
        entry = sa[j].astype(BF16)
        gdl[j] += dot_rows(hidden[j], entry)
        grad_pre = (dot(dl[j], entry) * slope[j]).astype(BF16)
        gur[j] += dot_rows(first[j], grad_pre)
        sb[j] = dot(ur[j], grad_pre)
        return carry

    lax.fori_loop(0, own, step, 0, unroll=2)
    for k in range(n):
        piece = sb[:, k * bi : (k + 1) * bi, :].reshape(own * bi, width).astype(BF16)
        outer[k] = piece
        (odd if k & 1 else even)[seq.index(k & ~1)] = dot(wd[k], piece).astype(BF16)


def outer_kernel(n, per_half, *refs):
    x, c = (refs[:n], refs[n : 2 * n]), (refs[2 * n : 3 * n], refs[3 * n : 4 * n])
    gf, second = refs[4 * n : 4 * n + 2], refs[4 * n + 2 : 4 * n + 4]
    mask, select = refs[4 * n + 4 : 4 * n + 6]
    out, acc_x, acc_c = refs[-3:]
    tile = pl.program_id(0)

    @pl.when(tile == 0)
    def _():
        acc_x[...] = jnp.zeros_like(acc_x)
        acc_c[...] = jnp.zeros_like(acc_c)

    for h in range(2):

        @pl.when(tile // per_half == h)
        def _():
            for k in range(n):
                acc_x[k] += dot_rows(gf[h][k], x[h][k][...])
                acc_c[k] += dot_rows(second[h][k], c[h][k][...])

    @pl.when(tile == 2 * per_half - 1)
    def _():
        me = lax.axis_index("block")
        for k in range(n):
            kept = mask[...]
            out[me ^ k] = (
                dot(acc_x[k].astype(BF16) * kept, select[0])
                + dot(acc_c[k].astype(BF16) * kept, select[1])
            ).astype(BF16)


def make_on_device(n, m):
    def on_device(tokens, up_left, up_right, down_left, down_right, cotangent):
        me = lax.axis_index("block")
        rows = tokens.shape[0]
        bi, aw, mb = up_left.shape
        own, bs = mb // n, up_right.shape[1]
        piece, ends, span = own * bi, bi * aw, rows // 2
        tiles = span // TILE

        outer = jnp.concatenate(
            [jnp.transpose(up_left, (2, 0, 1)), jnp.transpose(down_right, (1, 0, 2))], axis=2
        ).reshape(n, piece, 2 * aw)
        outer = lax.all_to_all(outer, "block", split_axis=0, concat_axis=0, tiled=True)
        lane, row = jnp.arange(ends), jnp.arange(piece)
        mask = (row[:, None] % bi == lane[None, :] // aw).astype(BF16)
        spread = lane[None, :] % aw == jnp.arange(2 * aw)[:, None] - jnp.array([[[0]], [[aw]]])
        spread = spread.astype(BF16)
        select = jnp.transpose(spread, (0, 2, 1))
        forms = (outer, spread, select, mask, mask.T)
        index = jnp.arange(bs)
        target = ((index // bi) ^ me) * bi + index % bi
        perm = (index[:, None] == target[None, :]).astype(BF16)
        ur = mul("jim,ip->jpm", up_right, perm).astype(BF16)
        dl = mul("jkl,lp->jkp", down_left, perm).astype(BF16)
        urt, dlt = jnp.transpose(ur, (0, 2, 1)), jnp.transpose(dl, (0, 2, 1))

        xt, ct = tokens.T, cotangent.T
        x = gather((xt[:, :span], xt[:, span:]), n)
        ct, *_ = lax.optimization_barrier(
            (ct, x[0][orders(n)[0][0]], x[1][orders(n)[1][0]])
        )
        c = gather((ct[:, :span], ct[:, span:]), n)

        ends_in = pl.BlockSpec((ends, TILE), lambda t: (0, t))
        middle = pl.BlockSpec((own, bs, TILE), lambda t: (0, 0, t))
        outside = pl.BlockSpec((n, piece, TILE), lambda t: (0, 0, t))
        parts = pl.BlockSpec((n // 2, ends, TILE), lambda t: (0, 0, t))
        square = pl.BlockSpec((own, bs, bs), lambda t: (0, 0, 0))
        middle_of = lambda kind: jax.ShapeDtypeStruct((own, bs, span), kind)
        outside_of = jax.ShapeDtypeStruct((n, piece, span), BF16)
        parts_of = jax.ShapeDtypeStruct((n // 2, ends, span), BF16)
        square_of = jax.ShapeDtypeStruct((own, bs, bs), F32)
        scratch = [pltpu.VMEM((own, bs, TILE), F32)] * 2
        flops = 2 * n * 2 * piece * ends * span + 4 * own * bs * bs * span
        cost = pl.CostEstimate(flops=flops, bytes_accessed=30_000_000, transcendentals=0)

        wide = [pltpu.VMEM((n, piece, ends), BF16), pltpu.VMEM((n, ends, piece), BF16)]
        later = pl.BlockSpec(memory_space=pl.ANY)
        bits = orders(n)

        def forward_half(h, after):
            return pl.pallas_call(
                functools.partial(forward_kernel, n, bi, own, sequence(n, h)),
                grid=(tiles,),
                in_specs=[ends_in] * n + [WHOLE] * 7 + [later] * len(after),
                out_specs=[middle, middle, middle, outside, parts, parts],
                out_shape=[
                    middle_of(BF16), middle_of(F32), middle_of(BF16), outside_of, parts_of, parts_of
                ],
                scratch_shapes=scratch + wide,
                compiler_params=PARAMS,
                cost_estimate=cost,
                name="forward_chain",
            )(*[x[h][k] for k in range(n)], *forms, urt, dlt, *after)

        def backward_half(h, after):
            return pl.pallas_call(
                functools.partial(backward_kernel, n, bi, own, sequence(n, h)),
                grid=(tiles,),
                in_specs=[ends_in] * n + [WHOLE] * 7 + [middle] * 3 + [later] * len(after),
                out_specs=[square, square, outside, parts, parts],
                out_shape=[square_of, square_of, outside_of, parts_of, parts_of],
                scratch_shapes=scratch + wide,
                compiler_params=PARAMS,
                cost_estimate=cost,
                name="backward_chain",
            )(*[c[h][k] for k in range(n)], *forms, ur, dl, first[h], slope[h], hidden[h], *after)

        f0 = forward_half(0, [])
        f1 = forward_half(1, [c[h][bits[h][0]] for h in range(2)])
        first, slope, hidden, second, even, odd = zip(f0, f1)
        out = [fold(even[h], odd[h], n, 1) for h in range(2)]
        b0 = backward_half(0, out)
        out = [scatter_step(out[h], n, bits[h][0]) for h in range(2)]
        b1 = backward_half(1, out)
        for step in range(1, len(bits[0])):
            out = [scatter_step(out[h], n, bits[h][step]) for h in range(2)]
        grad_dl, grad_ur, grad_first, even, odd = zip(b0, b1)
        gx = [fold(even[h], odd[h], n, 1) for h in range(2)]

        grad_dl = mul("jkp,lp->jkl", (grad_dl[0] + grad_dl[1]).astype(BF16), perm).astype(BF16)
        grad_ur = mul("jpm,ip->jim", (grad_ur[0] + grad_ur[1]).astype(BF16), perm).astype(BF16)
        squares, finish_squares = sum_groups(
            jnp.concatenate([grad_dl.reshape(-1, bs), grad_ur.reshape(-1, bs)], axis=0), m
        )

        ends_at = [
            pl.BlockSpec((ends, TILE), lambda t: (0, jnp.minimum(t, tiles - 1))),
            pl.BlockSpec((ends, TILE), lambda t: (0, jnp.maximum(t - tiles, 0))),
        ]
        outside_at = [
            pl.BlockSpec((n, piece, TILE), lambda t: (0, 0, jnp.minimum(t, tiles - 1))),
            pl.BlockSpec((n, piece, TILE), lambda t: (0, 0, jnp.maximum(t - tiles, 0))),
        ]
        both = pl.pallas_call(
            functools.partial(outer_kernel, n, tiles),
            grid=(2 * tiles,),
            in_specs=([ends_at[0]] * n + [ends_at[1]] * n) * 2 + outside_at * 2 + [WHOLE] * 2 + [later] * 4,
            out_specs=pl.BlockSpec((n, piece, 2 * aw), lambda t: (0, 0, 0)),
            out_shape=jax.ShapeDtypeStruct((n, piece, 2 * aw), BF16),
            scratch_shapes=[pltpu.VMEM((n, piece, ends), F32)] * 2,
            compiler_params=PARAMS,
            cost_estimate=cost,
            name="outer_gradients",
        )(
            *[x[h][k] for h in range(2) for k in range(n)],
            *[c[h][k] for h in range(2) for k in range(n)],
            *grad_first, *second, mask, select, *gx, *out,
        )
        for step in range(len(bits[0])):
            gx = [scatter_step(gx[h], n, bits[h][step]) for h in range(2)]
        both, squares = lax.optimization_barrier((both, squares))
        both = lax.all_to_all(both, "block", split_axis=0, concat_axis=0, tiled=True)
        both, finish_both = sum_groups(both.reshape(n * piece, 2 * aw), m)
        square_sum = finish_squares(squares).astype(F32).reshape(2, own, bs, bs)
        both = finish_both(both).reshape(mb, bi, 2 * aw).astype(F32)
        return (
            jnp.concatenate([out[0][0], out[1][0]], axis=1).T,
            jnp.concatenate([gx[0][0], gx[1][0]], axis=1).T,
            jnp.transpose(both[:, :, :aw], (1, 2, 0)),
            square_sum[1],
            square_sum[0],
            jnp.transpose(both[:, :, aw:], (1, 0, 2)),
        )

    return on_device


def solution(mesh):
    return jax.shard_map(
        make_on_device(mesh.shape["block"], mesh.shape["dp"]),
        mesh=mesh,
        in_specs=(
            P("dp", "block"),
            P("block", None, None),
            P("block", None, None),
            P("block", None, None),
            P("block", None, None),
            P("dp", "block"),
        ),
        out_specs=(
            P("dp", "block"),
            P("dp", "block"),
            P("block", None, None),
            P("block", None, None),
            P("block", None, None),
            P("block", None, None),
        ),
        check_vma=False,
    )
```

```python
import functools

import jax
import jax.numpy as jnp
from jax import lax
from jax.experimental import pallas as pl
from jax.experimental.pallas import tpu as pltpu
from jax.sharding import PartitionSpec as P

root_half = 0.7071067811865476
gauss_norm = 0.3989422804014327
F32, BF16 = jnp.float32, jnp.bfloat16
TILE = 256
WHOLE = pl.BlockSpec(memory_space=pltpu.VMEM)
PARAMS = pltpu.CompilerParams(vmem_limit_bytes=56 * 1024 * 1024)


def mul(spec, a, b):
    return jnp.einsum(spec, a, b, preferred_element_type=F32)


def dot(a, b):
    return jnp.dot(a, b, preferred_element_type=F32)


def dot_rows(a, b):
    return lax.dot_general(a, b, (((1,), (1,)), ((), ())), preferred_element_type=F32)


def swap(piece, n, bit):
    return lax.ppermute(piece, "block", [(d, d ^ bit) for d in range(n)])


def orders(n):
    bits = [1 << p for p in range(1, n.bit_length() - 1)]
    return bits, bits[::-1]


def sequence(n, h):
    seq = [0]
    for bit in orders(n)[h][::-1]:
        seq = seq + [k ^ bit for k in seq]
    return seq


def gather(halves, n, tied=False):
    have = [{0: half} for half in halves]
    for step in range(len(orders(n)[0])):
        if tied and step == 1:
            keys = [(h, k) for h in range(2) for k in have[h]]
            held = lax.optimization_barrier([have[h][k] for h, k in keys])
            for (h, k), value in zip(keys, held):
                have[h][k] = value
        for h, order in enumerate(orders(n)):
            for k in sorted(have[h]):
                have[h][k ^ order[step]] = swap(have[h][k], n, order[step])
    for h in range(2):
        for k in list(have[h]):
            have[h][k ^ 1] = swap(have[h][k], n, 1)
    return have


def fold(kept, sent, n, bit):
    return (kept.astype(F32) + swap(sent, n, bit).astype(F32)).astype(BF16)


def scatter_step(now, n, bit):
    middle = now.shape[0] // 2
    return fold(now[:middle], now[middle:], n, bit)


def sum_groups(rows, m):
    me = lax.axis_index("dp")
    bits = [1 << p for p in range(m.bit_length() - 1)]

    def trade(value, bit):
        return lax.ppermute(value, "dp", [(d, d ^ bit) for d in range(m)])

    def halve(value, bit):
        side = lax.rem(me // bit, 2)
        size = value.shape[0] // 2
        kept = lax.dynamic_slice_in_dim(value, side * size, size, 0)
        sent = lax.dynamic_slice_in_dim(value, (1 - side) * size, size, 0)
        return kept, trade(sent, bit)

    def add(kept, got):
        return (kept.astype(F32) + got.astype(F32)).astype(BF16)

    def finish(kept, got):
        value = add(kept, got)
        for bit in bits[1:]:
            value = add(*halve(value, bit))
        for bit in bits[::-1]:
            got, low = trade(value, bit), lax.rem(me // bit, 2) == 0
            value = jnp.concatenate([jnp.where(low, value, got), jnp.where(low, got, value)])
        return value

    return halve(rows, bits[0]), finish


def build(n, which_in, which_out, outer, spread, tall_spread, mask, tall_mask, wf, wd):
    me = lax.axis_index("block")
    for k in range(n):
        block = outer[me ^ k]
        wf[k] = dot(block, spread[which_in]).astype(BF16) * mask[...]
        wd[k] = dot_rows(tall_spread[which_out], block).astype(BF16) * tall_mask[...]


def forward_kernel(n, bi, own, seq, *refs):
    x = refs[:n]
    outer_in, spread, tall_spread, mask, tall_mask, urt, dlt = refs[n : n + 7]
    first, slope, hidden, outer, even, odd, sa, sb, wf, wd = refs[-10:]
    width = first.shape[2]

    @pl.when(pl.program_id(0) == 0)
    def _():
        build(n, 0, 1, outer_in, spread, tall_spread, mask, tall_mask, wf, wd)

    for k in range(n):
        sa[:, k * bi : (k + 1) * bi, :] = dot(wf[k], x[k][...]).reshape(own, bi, width)

    def step(j, carry):
        entry = sa[j].astype(BF16)
        first[j] = entry
        pre = dot(urt[j], entry)
        cdf = 0.5 * (1.0 + lax.erf(pre * root_half))
        slope[j] = cdf + pre * jnp.exp(-0.5 * pre * pre) * gauss_norm
        act = (pre * cdf).astype(BF16)
        hidden[j] = act
        sb[j] = dot(dlt[j], act)
        return carry

    lax.fori_loop(0, own, step, 0, unroll=2)
    for k in range(n):
        piece = sb[:, k * bi : (k + 1) * bi, :].reshape(own * bi, width).astype(BF16)
        outer[k] = piece
        (odd if k & 1 else even)[seq.index(k & ~1)] = dot(wd[k], piece).astype(BF16)


def backward_kernel(n, bi, own, seq, *refs):
    c = refs[:n]
    outer_in, spread, tall_spread, mask, tall_mask, ur, dl, first, slope, hidden = refs[n : n + 10]
    gdl, gur, outer, even, odd, sa, sb, wf, wd = refs[-9:]
    width = first.shape[2]

    @pl.when(pl.program_id(0) == 0)
    def _():
        gdl[...] = jnp.zeros_like(gdl)
        gur[...] = jnp.zeros_like(gur)
        build(n, 1, 0, outer_in, spread, tall_spread, mask, tall_mask, wf, wd)

    for k in range(n):
        sa[:, k * bi : (k + 1) * bi, :] = dot(wf[k], c[k][...]).reshape(own, bi, width)

    def step(j, carry):
        entry = sa[j].astype(BF16)
        gdl[j] += dot_rows(hidden[j], entry)
        grad_pre = (dot(dl[j], entry) * slope[j]).astype(BF16)
        gur[j] += dot_rows(first[j], grad_pre)
        sb[j] = dot(ur[j], grad_pre)
        return carry

    lax.fori_loop(0, own, step, 0, unroll=2)
    for k in range(n):
        piece = sb[:, k * bi : (k + 1) * bi, :].reshape(own * bi, width).astype(BF16)
        outer[k] = piece
        (odd if k & 1 else even)[seq.index(k & ~1)] = dot(wd[k], piece).astype(BF16)


def outer_kernel(n, per_half, *refs):
    x, c = (refs[:n], refs[n : 2 * n]), (refs[2 * n : 3 * n], refs[3 * n : 4 * n])
    gf, second = refs[4 * n : 4 * n + 2], refs[4 * n + 2 : 4 * n + 4]
    mask, select = refs[4 * n + 4 : 4 * n + 6]
    out, acc_x, acc_c = refs[-3:]
    tile = pl.program_id(0)

    @pl.when(tile == 0)
    def _():
        acc_x[...] = jnp.zeros_like(acc_x)
        acc_c[...] = jnp.zeros_like(acc_c)

    for h in range(2):

        @pl.when(tile // per_half == h)
        def _():
            for k in range(n):
                acc_x[k] += dot_rows(gf[h][k], x[h][k][...])
                acc_c[k] += dot_rows(second[h][k], c[h][k][...])

    @pl.when(tile == 2 * per_half - 1)
    def _():
        me = lax.axis_index("block")
        for k in range(n):
            kept = mask[...]
            out[me ^ k] = (
                dot(acc_x[k].astype(BF16) * kept, select[0])
                + dot(acc_c[k].astype(BF16) * kept, select[1])
            ).astype(BF16)


def make_on_device(n, m):
    def on_device(tokens, up_left, up_right, down_left, down_right, cotangent):
        me = lax.axis_index("block")
        rows = tokens.shape[0]
        bi, aw, mb = up_left.shape
        own, bs = mb // n, up_right.shape[1]
        piece, ends, span = own * bi, bi * aw, rows // 2
        tiles = span // TILE

        outer = jnp.concatenate(
            [jnp.transpose(up_left, (2, 0, 1)), jnp.transpose(down_right, (1, 0, 2))], axis=2
        ).reshape(n, piece, 2 * aw)
        outer = lax.all_to_all(outer, "block", split_axis=0, concat_axis=0, tiled=True)
        lane, row = jnp.arange(ends), jnp.arange(piece)
        mask = (row[:, None] % bi == lane[None, :] // aw).astype(BF16)
        spread = lane[None, :] % aw == jnp.arange(2 * aw)[:, None] - jnp.array([[[0]], [[aw]]])
        spread = spread.astype(BF16)
        select = jnp.transpose(spread, (0, 2, 1))
        forms = (outer, spread, select, mask, mask.T)
        index = jnp.arange(bs)
        target = ((index // bi) ^ me) * bi + index % bi
        perm = (index[:, None] == target[None, :]).astype(BF16)
        ur = mul("jim,ip->jpm", up_right, perm).astype(BF16)
        dl = mul("jkl,lp->jkp", down_left, perm).astype(BF16)
        urt, dlt = jnp.transpose(ur, (0, 2, 1)), jnp.transpose(dl, (0, 2, 1))

        xt, ct = tokens.T, cotangent.T
        x = gather((xt[:, :span], xt[:, span:]), n)
        ct, *_ = lax.optimization_barrier(
            (ct, x[0][orders(n)[0][0]], x[1][orders(n)[1][0]])
        )
        c = gather((ct[:, :span], ct[:, span:]), n, tied=True)

        ends_in = pl.BlockSpec((ends, TILE), lambda t: (0, t))
        middle = pl.BlockSpec((own, bs, TILE), lambda t: (0, 0, t))
        outside = pl.BlockSpec((n, piece, TILE), lambda t: (0, 0, t))
        parts = pl.BlockSpec((n // 2, ends, TILE), lambda t: (0, 0, t))
        square = pl.BlockSpec((own, bs, bs), lambda t: (0, 0, 0))
        middle_of = lambda kind: jax.ShapeDtypeStruct((own, bs, span), kind)
        outside_of = jax.ShapeDtypeStruct((n, piece, span), BF16)
        parts_of = jax.ShapeDtypeStruct((n // 2, ends, span), BF16)
        square_of = jax.ShapeDtypeStruct((own, bs, bs), F32)
        scratch = [pltpu.VMEM((own, bs, TILE), F32)] * 2
        flops = 2 * n * 2 * piece * ends * span + 4 * own * bs * bs * span
        cost = pl.CostEstimate(flops=flops, bytes_accessed=30_000_000, transcendentals=0)

        wide = [pltpu.VMEM((n, piece, ends), BF16), pltpu.VMEM((n, ends, piece), BF16)]
        later = pl.BlockSpec(memory_space=pl.ANY)
        bits = orders(n)

        def forward_half(h, after):
            return pl.pallas_call(
                functools.partial(forward_kernel, n, bi, own, sequence(n, h)),
                grid=(tiles,),
                in_specs=[ends_in] * n + [WHOLE] * 7 + [later] * len(after),
                out_specs=[middle, middle, middle, outside, parts, parts],
                out_shape=[
                    middle_of(BF16), middle_of(F32), middle_of(BF16), outside_of, parts_of, parts_of
                ],
                scratch_shapes=scratch + wide,
                compiler_params=PARAMS,
                cost_estimate=cost,
                name="forward_chain",
            )(*[x[h][k] for k in range(n)], *forms, urt, dlt, *after)

        def backward_half(h, after):
            return pl.pallas_call(
                functools.partial(backward_kernel, n, bi, own, sequence(n, h)),
                grid=(tiles,),
                in_specs=[ends_in] * n + [WHOLE] * 7 + [middle] * 3 + [later] * len(after),
                out_specs=[square, square, outside, parts, parts],
                out_shape=[square_of, square_of, outside_of, parts_of, parts_of],
                scratch_shapes=scratch + wide,
                compiler_params=PARAMS,
                cost_estimate=cost,
                name="backward_chain",
            )(*[c[h][k] for k in range(n)], *forms, ur, dl, first[h], slope[h], hidden[h], *after)

        near = [c[h][bits[h][0]] for h in range(2)]
        f0 = forward_half(0, near)
        early = [c[h][k] for h in range(2) for k in c[h] if k != bits[h][0]]
        late = [c[h][k ^ 1] for h in range(2) for k in c[h] if k and k != bits[h][0] and not k & 1]
        f1 = forward_half(1, [e for e in early if not any(e is item for item in late)])
        first, slope, hidden, second, even, odd = zip(f0, f1)
        out = [fold(even[h], odd[h], n, 1) for h in range(2)]
        b0 = backward_half(0, out)
        out = [scatter_step(out[h], n, bits[h][0]) for h in range(2)]
        b1 = backward_half(1, out)
        for step in range(1, len(bits[0])):
            out = [scatter_step(out[h], n, bits[h][step]) for h in range(2)]
        grad_dl, grad_ur, grad_first, even, odd = zip(b0, b1)
        gx = [fold(even[h], odd[h], n, 1) for h in range(2)]

        grad_dl = mul("jkp,lp->jkl", (grad_dl[0] + grad_dl[1]).astype(BF16), perm).astype(BF16)
        grad_ur = mul("jpm,ip->jim", (grad_ur[0] + grad_ur[1]).astype(BF16), perm).astype(BF16)
        squares, finish_squares = sum_groups(
            jnp.concatenate([grad_dl.reshape(-1, bs), grad_ur.reshape(-1, bs)], axis=0), m
        )

        ends_at = [
            pl.BlockSpec((ends, TILE), lambda t: (0, jnp.minimum(t, tiles - 1))),
            pl.BlockSpec((ends, TILE), lambda t: (0, jnp.maximum(t - tiles, 0))),
        ]
        outside_at = [
            pl.BlockSpec((n, piece, TILE), lambda t: (0, 0, jnp.minimum(t, tiles - 1))),
            pl.BlockSpec((n, piece, TILE), lambda t: (0, 0, jnp.maximum(t - tiles, 0))),
        ]
        both = pl.pallas_call(
            functools.partial(outer_kernel, n, tiles),
            grid=(2 * tiles,),
            in_specs=([ends_at[0]] * n + [ends_at[1]] * n) * 2 + outside_at * 2 + [WHOLE] * 2 + [later] * 4,
            out_specs=pl.BlockSpec((n, piece, 2 * aw), lambda t: (0, 0, 0)),
            out_shape=jax.ShapeDtypeStruct((n, piece, 2 * aw), BF16),
            scratch_shapes=[pltpu.VMEM((n, piece, ends), F32)] * 2,
            compiler_params=PARAMS,
            cost_estimate=cost,
            name="outer_gradients",
        )(
            *[x[h][k] for h in range(2) for k in range(n)],
            *[c[h][k] for h in range(2) for k in range(n)],
            *grad_first, *second, mask, select, *gx, *out,
        )
        center = gx[0].shape[0] // 2
        got = [swap(gx[h][center:], n, bits[h][0]) for h in range(2)]
        got, squares, both = lax.optimization_barrier((got, squares, both))
        both = lax.all_to_all(both, "block", split_axis=0, concat_axis=0, tiled=True)
        gx = [(gx[h][:center].astype(F32) + got[h].astype(F32)).astype(BF16) for h in range(2)]
        gx, squares, both = lax.optimization_barrier((gx, squares, both))
        for step in range(1, len(bits[0])):
            gx = [scatter_step(gx[h], n, bits[h][step]) for h in range(2)]
        both, finish_both = sum_groups(both.reshape(n * piece, 2 * aw), m)
        square_sum = finish_squares(*squares).astype(F32).reshape(2, own, bs, bs)
        both = finish_both(*both).reshape(mb, bi, 2 * aw).astype(F32)
        return (
            jnp.concatenate([out[0][0], out[1][0]], axis=1).T,
            jnp.concatenate([gx[0][0], gx[1][0]], axis=1).T,
            jnp.transpose(both[:, :, :aw], (1, 2, 0)),
            square_sum[1],
            square_sum[0],
            jnp.transpose(both[:, :, aw:], (1, 0, 2)),
        )

    return on_device


def solution(mesh):
    return jax.shard_map(
        make_on_device(mesh.shape["block"], mesh.shape["dp"]),
        mesh=mesh,
        in_specs=(
            P("dp", "block"),
            P("block", None, None),
            P("block", None, None),
            P("block", None, None),
            P("block", None, None),
            P("dp", "block"),
        ),
        out_specs=(
            P("dp", "block"),
            P("dp", "block"),
            P("block", None, None),
            P("block", None, None),
            P("block", None, None),
            P("block", None, None),
        ),
        check_vma=False,
    )
```
